32 devices in a mesh: groups: 2 (over x), dp: 16 (over z, y, core).
Axes of the slice: x: 2, y: 2, z: 4, core: 2. Of those that a mesh axis runs over, the one named last changes fastest.
Arguments:
- tokens: bfloat16 [4096, 2048], P(('groups', 'dp')), parts along dimension 0, may hold values from -6 to 6
- mask_positions: int32 [4096], P(('groups', 'dp')), parts along dimension 0, may hold values 0 or 1
- mask_embed: bfloat16 [2048], replicated, may hold values from -6 to 6
- queries: bfloat16 [4096, 2048], P(('groups', 'dp')), parts along dimension 0, may hold values from -70 to 70
- new_keys: bfloat16 [4096, 256], P(('groups', 'dp')), parts along dimension 0, may hold values from -10 to 10
- new_values: bfloat16 [4096, 256], P(('groups', 'dp')), parts along dimension 0, may hold values from -10 to 10
- cache_keys: bfloat16 [128, 1024, 256], P(('groups', 'dp')), parts along dimension 0, may hold values from -12 to 12
- cache_values: bfloat16 [128, 1024, 256], P(('groups', 'dp')), parts along dimension 0, may hold values from -10 to 10
- prefix_lengths: int32 [128], P(('groups', 'dp')), parts along dimension 0, may hold values from 2 to 1024, as said below
- expert_ids: int32 [4096, 8], P(('groups', 'dp')), parts along dimension 0, may hold values from 0 to 15, all different within a row; in each aligned block of 128 rows (0 to 127, 128 to 255, ...) at most 72 rows name the same one
- gate_probs: float32 [4096, 8], P(('groups', 'dp')), parts along dimension 0, may hold values from 0.05 to 0.5
- norm_gain: bfloat16 [2048], replicated, may hold values from 0.099609375 to 1.8984375
- gate_quant: bfloat16 [16, 2048, 512], P('dp'), may hold values from -0.125 to 0.125
- gate_scale: float32 [16, 16, 4], P('dp'), may hold values from 0.3 to 3
- up_quant: bfloat16 [16, 2048, 512], P('dp'), may hold values from -0.125 to 0.125
- up_scale: float32 [16, 16, 4], P('dp'), may hold values from 0.3 to 3
- down_quant: bfloat16 [16, 512, 2048], P('dp'), may hold values from -0.25 to 0.25
- down_scale: float32 [16, 4, 16], P('dp'), may hold values from 0.3 to 3
Outputs:
- mixed: bfloat16 [4096, 2048], P(('groups', 'dp')), parts along dimension 0
The draws below stay inside these ranges and needn't reach their ends.
There are 2 independent parts, one for each index of `groups`. The reference program is written for one: setup_inputs(seed, part) draws one part's arguments, and reference() takes and returns one part's arrays. A program takes and returns all parts, laid end to end along the dimension named above; an argument that names none is the same for every part. Nothing has to cross between parts.
Inputs may be any that keep to these rules, and one draw needn't show every extreme that they name: `expert_ids`: each row names 8 different experts; in the 128 rows of one device no expert is named by more than 72 rows. `prefix_lengths`: some request has exactly 1024 cached tokens.
All inputs are finite; a program needn't handle non-finite values. No bound on the sum of `mask_positions` on one device may be relied on, other than what follows from the above.
Results may differ from the reference program's by a relative error of at most 0.017.
Values may be sent and summed in bfloat16 or wider, within the bound.
No kernel may reach another device: no remote copies, remote signals or barrier semaphores. Data moves between devices by JAX's collectives and lax.ppermute only.
A program may use at most 128 MiB of HBM per device.

```python
import math
import jax
import jax.numpy as jnp
import numpy as np
from jax import lax

D = 2048
HQ = 16
HK = 2
HD = 128
FF_E = 512
QB = 128
TOPK = 8
BLOCK = 32
PREFIX = 1024
TOK_DEV = 128
REQS = 64
TOKENS = 2048
EXPERTS = 16
CAP = 72
N_DP = 16


def shared_keys(key):
    base = jax.random.normal(jax.random.fold_in(key, 41), (REQS, PREFIX, HK * HD), jnp.float32)
    return jnp.clip(base, -5.0, 5.0)


def draw_cache_keys(key, part):
    base = shared_keys(key)
    keys = 2.0 * base
    return keys.astype(jnp.bfloat16)


def draw_queries(key, part):
    key = jax.random.fold_in(key, 7)
    first = jax.random.fold_in(key, 0)
    values = jnp.clip(jax.random.normal(first, (TOKENS, D), jnp.float32), -5.0, 5.0)
    return values.astype(jnp.bfloat16)


def draw_prefix_lengths(key, part):
    key = jax.random.fold_in(key, 5)
    first, second, third = jax.random.split(key, 3)
    left = jax.random.randint(first, (REQS,), 0, PREFIX - 1)
    right = jax.random.randint(second, (REQS,), 0, PREFIX - 1)
    lengths = 2 + left * right // PREFIX
    longest = jax.random.randint(third, (), 0, REQS)
    return lengths.at[longest].set(PREFIX).astype(jnp.int32)


def set_ends(array, key, smallest, largest):
    extent = array.shape
    place = [jax.random.randint(jax.random.fold_in(key, axis), (), 0, extent[axis]) for axis in range(len(extent))]
    array = array.at[tuple(place)].set(smallest)
    longest = extent.index(max(extent))
    place[longest] = (place[longest] + 1) % extent[longest]
    return array.at[tuple(place)].set(largest)


def block_levels(own_key, extent, cuts, least, top_value):
    def one(axis_at, blocks):
        heights = jax.random.uniform(jax.random.fold_in(jax.random.fold_in(own_key, 6), axis_at), (blocks,), jnp.float32, least / len(cuts), top_value / len(cuts))
        return jnp.repeat(jnp.exp(heights), extent[axis_at] // blocks).reshape((-1,) + (1,) * (len(extent) - axis_at - 1))

    loudness = one(*cuts[0])
    for cut in cuts[1:]:
        loudness = loudness * one(*cut)
    return loudness


def routed_block(stream_key, own, number, rows, amount, top, reach, slope):
    ranking = jax.random.permutation(stream_key, amount)
    packed, usual = shares(amount, rows * top, reach, slope, True), shares(amount, rows * top, reach, slope, False)
    places = jnp.arange(amount)

    def named(tallies, turn):
        used = int((tallies > 0).sum())
        fixed = max(1, used // 4)
        moved = fixed + (places - fixed + turn * (used - fixed)) % max(1, amount - fixed)
        return jnp.zeros((amount,), jnp.int32).at[ranking[jnp.where(places < fixed, places, moved)]].set(jnp.asarray(tallies, jnp.int32))

    tallies = jnp.where(number % 4 == 0, named(packed, number // 4), named(usual, number - number // 4 - 1))
    mixed = jax.random.permutation(jax.random.fold_in(own, 3), amount)
    source_of, sink = mixed[0:amount // 2 * 2:2], mixed[1:amount // 2 * 2:2]
    slack = jnp.minimum(tallies[source_of] - 1, reach - tallies[sink]) // 2
    slack = jnp.where((source_of == ranking[0]) | (sink == ranking[0]) | (tallies[sink] == 0), 0, jnp.maximum(slack, 0))
    moved = jax.random.randint(jax.random.fold_in(own, 4), (amount // 2,), 0, 1 << 20) % (slack + 1)
    tallies = tallies.at[source_of].add(-moved).at[sink].add(moved)
    items = jnp.searchsorted(jnp.cumsum(tallies), jnp.arange(rows * top), side="right").astype(jnp.int32)
    listing = items.reshape(top, rows).T
    listing = listing[jax.random.permutation(jax.random.fold_in(own, 1), rows)]
    turn = jax.random.randint(jax.random.fold_in(own, 2), (rows, 1), 0, top)
    return jnp.take_along_axis(listing, (jnp.arange(top)[None, :] + turn) % top, axis=1)


def shares(number_of, total, reach, skew, full):
    loads = [(1 << 20) // math.isqrt(grade ** skew) + 1 for grade in range(1, number_of + 1)]
    largest = reach if full else min(reach, max(-(-total // number_of), total * loads[0] // sum(loads)))
    least = 1 if total - largest >= number_of - 1 else 0
    given, surplus = [largest] + [least] * (number_of - 1), total - largest - least * (number_of - 1)
    while surplus > 0:
        movable = [i for i in range(1, number_of) if given[i] < largest] or [i for i in range(1, number_of) if given[i] < reach]
        mass, left = sum([loads[i] for i in movable]), surplus
        for i in movable:
            addition = min(reach - given[i], max(1, left * loads[i] // mass), surplus)
            given[i] = given[i] + addition
            surplus = surplus - addition
    return np.array(given)


def scatter_about(rng, extent, deviation, reach, cuts=(), kind=jnp.bfloat16):
    factor_of = block_levels(rng, extent, cuts, -0.22, 0.18) if cuts else 1.0
    values = jax.random.normal(rng, extent, jnp.float32) * deviation * factor_of
    return jnp.minimum(jnp.maximum(values, -reach), reach).astype(kind)


def setup_inputs(seed: int = 0, part: int = 0) -> dict:
    seeds = jax.random.split(jax.random.key(seed), 19)
    own_keys = jax.random.split(jax.random.fold_in(seeds[18], part), 19)
    tokens = scatter_about(own_keys[0], (TOKENS, D), 0.5, 6.0, ((0, 16),))
    mask_positions = set_ends((jax.random.randint(own_keys[1], (TOKENS,), 0, 2) < 1).astype(jnp.int32), jax.random.fold_in(own_keys[1], 1), 0, 1)
    mask_embed = scatter_about(seeds[2], (D,), 0.5, 6.0)
    queries = draw_queries(jax.random.fold_in(jax.random.fold_in(seeds[18], part), 71), part)
    new_keys = scatter_about(own_keys[4], (TOKENS, HK * HD), 2.0, 10.0, ((0, 16),))
    new_values = scatter_about(own_keys[5], (TOKENS, HK * HD), 2.0, 10.0, ((0, 16),))
    cache_keys = draw_cache_keys(jax.random.fold_in(jax.random.fold_in(seeds[18], part), 71), part)
    cache_values = scatter_about(own_keys[7], (REQS, PREFIX, HK * HD), 2.0, 10.0, ((0, 16),))
    prefix_lengths = draw_prefix_lengths(jax.random.fold_in(jax.random.fold_in(seeds[18], part), 71), part)
    expert_ids_keys = jax.random.split(jax.random.fold_in(own_keys[9], 1), TOKENS // TOK_DEV)
    expert_ids_turns = jax.random.permutation(jax.random.fold_in(own_keys[9], 3), TOKENS // TOK_DEV)
    expert_ids = jax.vmap(lambda own, number: routed_block(jax.random.fold_in(own_keys[9], 2), own, number, TOK_DEV, EXPERTS, TOPK, CAP, 1))(expert_ids_keys, expert_ids_turns).reshape((TOKENS, TOPK))
    gate_probs = jnp.clip(jnp.exp(math.log(0.5) - 2.3025851 * jax.random.uniform(own_keys[10], (TOKENS, TOPK), jnp.float32) ** block_levels(own_keys[10], (TOKENS, TOPK), ((0, 16),), -0.2, 0.2)), 0.05, 0.5)
    norm_gain = jnp.clip(1.0 + 0.18 * jax.random.normal(seeds[11], (D,), jnp.float32), 0.099609375, 1.8984375).astype(jnp.bfloat16)
    gate_quant = scatter_about(seeds[12], (EXPERTS, D, FF_E), D ** -0.5, 0.125, ((0, 16),))
    gate_scale = jnp.clip(jnp.exp(math.log(3.0) - 2.3025851 * jax.random.uniform(seeds[13], (EXPERTS, D // QB, FF_E // QB), jnp.float32) ** block_levels(seeds[13], (EXPERTS, D // QB, FF_E // QB), ((0, 16),), -0.2, 0.2)), 0.3, 3.0)
    up_quant = scatter_about(seeds[14], (EXPERTS, D, FF_E), D ** -0.5, 0.125, ((0, 16),))
    up_scale = jnp.clip(jnp.exp(math.log(3.0) - 2.3025851 * jax.random.uniform(seeds[15], (EXPERTS, D // QB, FF_E // QB), jnp.float32) ** block_levels(seeds[15], (EXPERTS, D // QB, FF_E // QB), ((0, 16),), -0.2, 0.2)), 0.3, 3.0)
    down_quant = scatter_about(seeds[16], (EXPERTS, FF_E, D), FF_E ** -0.5, 0.25, ((0, 16),))
    down_scale = jnp.clip(jnp.exp(math.log(3.0) - 2.3025851 * jax.random.uniform(seeds[17], (EXPERTS, FF_E // QB, D // QB), jnp.float32) ** block_levels(seeds[17], (EXPERTS, FF_E // QB, D // QB), ((0, 16),), -0.2, 0.2)), 0.3, 3.0)
    return {"tokens": tokens, "mask_positions": mask_positions, "mask_embed": mask_embed, "queries": queries, "new_keys": new_keys, "new_values": new_values, "cache_keys": cache_keys, "cache_values": cache_values, "prefix_lengths": prefix_lengths, "expert_ids": expert_ids, "gate_probs": gate_probs, "norm_gain": norm_gain, "gate_quant": gate_quant, "gate_scale": gate_scale, "up_quant": up_quant, "up_scale": up_scale, "down_quant": down_quant, "down_scale": down_scale}


def dequant(quantized, block_scale):
    row_count, col_count = quantized.shape
    blocks = quantized.astype(jnp.float32).reshape(row_count // QB, QB, col_count // QB, QB)
    blocks = blocks * block_scale[:, None, :, None]
    return blocks.reshape(row_count, col_count).astype(jnp.bfloat16)

def reference(tokens, mask_positions, mask_embed, queries, new_keys, new_values, cache_keys, cache_values, prefix_lengths, expert_ids, gate_probs, norm_gain, gate_quant, gate_scale, up_quant, up_scale, down_quant, down_scale):
    head_group = HQ // HK
    inputs = jnp.where(mask_positions[:, None] == 1, mask_embed[None, :], tokens)

    def attend(operands):
        query_rows, key_rows, value_rows, cached_keys, cached_values, length = operands
        query_heads = query_rows.astype(jnp.float32).reshape(BLOCK, HK, head_group, HD)
        all_keys = jnp.concatenate([cached_keys, key_rows], 0).astype(jnp.float32).reshape(PREFIX + BLOCK, HK, HD)
        all_values = jnp.concatenate([cached_values, value_rows], 0).astype(jnp.float32).reshape(PREFIX + BLOCK, HK, HD)
        scores = jnp.einsum('bkgd,pkd->kgbp', query_heads, all_keys) * (1.0 / math.sqrt(HD))
        position = jnp.arange(PREFIX + BLOCK)
        live_keys = (position < length) | (position >= PREFIX)
        scores = jnp.where(live_keys, scores, -1e+30)
        row_top = lax.optimization_barrier(jnp.max(scores, -1, keepdims=True))
        expo = jnp.where(live_keys, jnp.exp(scores - row_top), 0.0)
        probs = (expo / lax.optimization_barrier(jnp.sum(expo, -1, keepdims=True))).astype(jnp.bfloat16)
        weighted = jnp.einsum('kgbp,pkd->bkgd', probs.astype(jnp.float32), all_values)
        return weighted.reshape(BLOCK, D).astype(jnp.bfloat16)
    attended = lax.map(attend, (queries.reshape(REQS, BLOCK, D), new_keys.reshape(REQS, BLOCK, HK * HD), new_values.reshape(REQS, BLOCK, HK * HD), cache_keys, cache_values, prefix_lengths))
    attended = attended.reshape(TOKENS, D)
    resid = inputs.astype(jnp.float32) + attended.astype(jnp.float32)
    mean_square = lax.optimization_barrier(jnp.mean(resid * resid, -1, keepdims=True))
    normed = (resid * lax.rsqrt(mean_square + 1e-06) * norm_gain.astype(jnp.float32)).astype(jnp.bfloat16)
    device_ids = expert_ids.reshape(N_DP, TOK_DEV * TOPK)
    onehot = (device_ids[..., None] == jnp.arange(EXPERTS, dtype=jnp.int32)).astype(jnp.int32)
    before = jnp.cumsum(onehot, 1) - onehot
    slot_rank = lax.optimization_barrier(jnp.sum(before * onehot, -1))
    slot_index = (jnp.arange(N_DP, dtype=jnp.int32)[:, None] * CAP + slot_rank).reshape(TOKENS, TOPK).astype(jnp.int32)
    slot_count = N_DP * CAP

    def expert_pass(accum, expert):
        hit = expert_ids == expert
        has_slot = jnp.any(hit, 1)
        token_slot = lax.optimization_barrier(jnp.sum(jnp.where(hit, slot_index, 0), 1)).astype(jnp.int32)
        weight_sum = lax.optimization_barrier(jnp.sum(jnp.where(hit, gate_probs, 0.0), 1))
        target = jnp.where(has_slot, token_slot, slot_count).astype(jnp.int32)
        buffer = jnp.zeros((slot_count, D), jnp.bfloat16).at[target].set(normed, mode='drop')
        w_gate = dequant(gate_quant[expert], gate_scale[expert])
        w_up = dequant(up_quant[expert], up_scale[expert])
        w_down = dequant(down_quant[expert], down_scale[expert])
        gate_part = jnp.dot(buffer, w_gate, preferred_element_type=jnp.float32)
        up_part = jnp.dot(buffer, w_up, preferred_element_type=jnp.float32)
        hidden = (jax.nn.silu(gate_part) * up_part).astype(jnp.bfloat16)
        result = jnp.dot(hidden, w_down, preferred_element_type=jnp.float32).astype(jnp.bfloat16)
        picked = result[jnp.minimum(token_slot, slot_count - 1)]
        return (accum + weight_sum[:, None] * picked.astype(jnp.float32), None)
    routed, _ = lax.scan(expert_pass, jnp.zeros((TOKENS, D), jnp.float32), jnp.arange(EXPERTS, dtype=jnp.int32))
    return (resid + routed).astype(jnp.bfloat16)
```

```python
import functools
import math

import jax
import jax.numpy as jnp
from jax import lax
from jax.experimental import pallas as pl
from jax.experimental.pallas import tpu as pltpu
from jax.sharding import PartitionSpec as P

HD = 128
QB = 128
BF16 = jnp.bfloat16
F32 = jnp.float32
VMEM_BYTES = 48 * 1024 * 1024


def params():
    return pltpu.CompilerParams(vmem_limit_bytes=VMEM_BYTES)


def attend_body(
    first,
    lens_ref,
    tok_ref,
    mask_ref,
    embed_ref,
    query_ref,
    new_key_ref,
    new_value_ref,
    key_ref,
    value_ref,
    gain_ref,
    resid_ref,
    normed_ref,
):
    block_len, width = tok_ref.shape
    prefix, kv_width = key_ref.shape[1:]
    kv_heads = kv_width // HD
    group = width // HD // kv_heads
    length = lens_ref[first + pl.program_id(0)]
    scale = 1.0 / math.sqrt(HD)
    contract_last = (((1,), (1,)), ((), ()))
    chosen = jnp.where(
        mask_ref[...] == 1, embed_ref[...].astype(F32), tok_ref[...].astype(F32)
    )
    pieces = []
    for head in range(kv_heads):
        lanes = slice(head * HD, (head + 1) * HD)
        query = jnp.concatenate(
            [
                query_ref[:, (head * group + g) * HD : (head * group + g + 1) * HD]
                for g in range(group)
            ],
            axis=0,
        )
        far = lax.dot_general(
            query, key_ref[0, :, lanes], contract_last, preferred_element_type=F32
        )
        near = lax.dot_general(
            query, new_key_ref[:, lanes], contract_last, preferred_element_type=F32
        )
        far = far * scale
        near = near * scale
        position = lax.broadcasted_iota(jnp.int32, far.shape, 1)
        far = jnp.where(position < length, far, -1e30)
        top = jnp.maximum(
            jnp.max(far, axis=1, keepdims=True), jnp.max(near, axis=1, keepdims=True)
        )
        far = jnp.exp(far - top)
        near = jnp.exp(near - top)
        total = jnp.sum(far, axis=1, keepdims=True) + jnp.sum(near, axis=1, keepdims=True)
        out = jnp.dot(far.astype(BF16), value_ref[0, :, lanes], preferred_element_type=F32)
        out = out + jnp.dot(
            near.astype(BF16), new_value_ref[:, lanes], preferred_element_type=F32
        )
        out = (out / total).astype(BF16).astype(F32)
        pieces += [out[g * block_len : (g + 1) * block_len] for g in range(group)]
    resid = chosen + jnp.concatenate(pieces, axis=1)
    mean_square = jnp.mean(resid * resid, axis=1, keepdims=True)
    resid_ref[...] = resid
    normed_ref[...] = (
        resid * lax.rsqrt(mean_square + 1e-06) * gain_ref[...].astype(F32)
    ).astype(BF16)


def attend(first, count, lens, tokens, mask, embed, queries, new_keys, new_values, keys, values, gain):
    tok_rows, width = tokens.shape
    requests, prefix, kv_width = keys.shape
    block_len = tok_rows // requests

    def rows(cols):
        return pl.BlockSpec((block_len, cols), lambda i, lens: (first + i, 0))

    def cache():
        return pl.BlockSpec((1, prefix, kv_width), lambda i, lens: (first + i, 0, 0))

    def whole(cols):
        return pl.BlockSpec((1, cols), lambda i, lens: (0, 0))

    out = pl.BlockSpec((block_len, width), lambda i, lens: (i, 0))
    scored = count * block_len * width * (prefix + block_len)
    return pl.pallas_call(
        functools.partial(attend_body, first),
        grid_spec=pltpu.PrefetchScalarGridSpec(
            num_scalar_prefetch=1,
            grid=(count,),
            in_specs=[
                rows(width),
                rows(1),
                whole(width),
                rows(width),
                rows(kv_width),
                rows(kv_width),
                cache(),
                cache(),
                whole(width),
            ],
            out_specs=[out, out],
        ),
        out_shape=[
            jax.ShapeDtypeStruct((count * block_len, width), F32),
            jax.ShapeDtypeStruct((count * block_len, width), BF16),
        ],
        compiler_params=params(),
        cost_estimate=pl.CostEstimate(
            flops=4 * scored,
            bytes_accessed=count * (4 * prefix * kv_width + 12 * block_len * width),
            transcendentals=scored // HD,
        ),
        name="attend",
    )(lens, tokens, mask, embed, queries, new_keys, new_values, keys, values, gain)


def scale_blocks(scale_ref, row_at, quant_ref, put):
    row_count, col_count = quant_ref.shape
    for i in range(row_count // QB):
        for j in range(col_count // QB):
            rows, cols = slice(i * QB, (i + 1) * QB), slice(j * QB, (j + 1) * QB)
            factor = scale_ref[row_at + i, j]
            put(rows, cols, (quant_ref[rows, cols].astype(F32) * factor).astype(BF16))


def dequant_body(gs_ref, us_ref, ds_ref, gate_ref, up_ref, down_ref, gate_up_ref, out_down_ref):
    step = pl.program_id(0)

    def put_gate(rows, cols, block):
        gate_up_ref[0, rows, cols] = block

    def put_up(rows, cols, block):
        gate_up_ref[1, rows, cols] = block

    def put_down(rows, cols, block):
        out_down_ref[rows, cols] = block

    scale_blocks(gs_ref, step * (gate_ref.shape[0] // QB), gate_ref, put_gate)
    scale_blocks(us_ref, step * (up_ref.shape[0] // QB), up_ref, put_up)
    scale_blocks(ds_ref, step * (down_ref.shape[0] // QB), down_ref, put_down)


def dequant(gate, gate_scale, up, up_scale, down, down_scale):
    width, hidden = gate.shape
    steps = hidden // QB
    part, down_part = width // steps, hidden // steps
    smem = pl.BlockSpec(memory_space=pltpu.SMEM)
    wide = pl.BlockSpec((part, hidden), lambda i: (i, 0))
    return pl.pallas_call(
        dequant_body,
        grid=(steps,),
        in_specs=[
            smem,
            smem,
            smem,
            wide,
            wide,
            pl.BlockSpec((down_part, width), lambda i: (i, 0)),
        ],
        out_specs=[
            pl.BlockSpec((2, part, hidden), lambda i: (0, i, 0)),
            pl.BlockSpec((down_part, width), lambda i: (i, 0)),
        ],
        out_shape=[
            jax.ShapeDtypeStruct((2, width, hidden), BF16),
            jax.ShapeDtypeStruct((hidden, width), BF16),
        ],
        compiler_params=params(),
        cost_estimate=pl.CostEstimate(
            flops=3 * width * hidden, bytes_accessed=12 * width * hidden, transcendentals=0
        ),
        name="dequant",
    )(gate_scale, up_scale, down_scale, gate, up, down)


def experts_body(blocks, tiles, *refs):
    x_refs, refs = refs[:blocks], refs[blocks:]
    weight_ref, own_gate_up, own_down, other_gate_up, other_down = refs[:5]
    out_refs = refs[5 : 5 + blocks]
    x_all, total = refs[5 + blocks :]
    step = pl.program_id(0)
    block_rows = x_refs[0].shape[0]

    @pl.when(step == 0)
    def _():
        for at, ref in enumerate(x_refs):
            x_all[at * block_rows : (at + 1) * block_rows] = ref[...]

    def tile(gate_up, down, column):
        rows = x_all[...]
        gate = jnp.dot(rows, gate_up[0], preferred_element_type=F32)
        up = jnp.dot(rows, gate_up[1], preferred_element_type=F32)
        hidden = gate * jax.nn.sigmoid(gate) * up * weight_ref[:, column : column + 1]
        return jnp.dot(hidden.astype(BF16), down[...], preferred_element_type=F32)

    @pl.when(step == 0)
    def _():
        total[...] = tile(own_gate_up, own_down, 0)

    @pl.when((step > 0) & (step < tiles))
    def _():
        total[...] += tile(own_gate_up, own_down, 0)

    @pl.when((step >= tiles) & (step < 2 * tiles - 1))
    def _():
        total[...] += tile(other_gate_up, other_down, 1)

    @pl.when(step == 2 * tiles - 1)
    def _():
        sums = (total[...] + tile(other_gate_up, other_down, 1)).astype(BF16)
        for at, ref in enumerate(out_refs):
            ref[...] = sums[at * block_rows : (at + 1) * block_rows]


def experts(xs, weights, own, other):
    rows, width = xs[0].shape
    hidden = own[0].shape[2]
    tile = min(256, hidden)
    tiles = hidden // tile
    blocks = len(xs)
    all_rows = rows * blocks

    def fixed(shape):
        return pl.BlockSpec(shape, lambda i: (0, 0))

    def first(i):
        return jnp.minimum(i, tiles - 1)

    def second(i):
        return jnp.maximum(i - tiles, 0)

    def pair(at):
        return [
            pl.BlockSpec((2, width, tile), lambda i: (0, 0, at(i))),
            pl.BlockSpec((tile, width), lambda i: (at(i), 0)),
        ]

    return pl.pallas_call(
        functools.partial(experts_body, blocks, tiles),
        grid=(2 * tiles,),
        in_specs=[fixed((rows, width))] * blocks
        + [fixed((all_rows, 2))]
        + pair(first)
        + pair(second),
        out_specs=[fixed((rows, width))] * blocks,
        out_shape=[jax.ShapeDtypeStruct((rows, width), BF16)] * blocks,
        scratch_shapes=[pltpu.VMEM((all_rows, width), BF16), pltpu.VMEM((all_rows, width), F32)],
        compiler_params=params(),
        cost_estimate=pl.CostEstimate(
            flops=12 * all_rows * width * hidden,
            bytes_accessed=12 * width * hidden + 4 * all_rows * width,
            transcendentals=2 * all_rows * hidden,
        ),
        name="experts",
    )(*xs, weights, *own, *other)


def add(*terms):
    total = terms[0].astype(F32)
    for term in terms[1:]:
        total = total + term.astype(F32)
    return total.astype(BF16)


def shards(
    sizes,
    tokens,
    mask_positions,
    mask_embed,
    queries,
    new_keys,
    new_values,
    cache_keys,
    cache_values,
    prefix_lengths,
    expert_ids,
    gate_probs,
    norm_gain,
    gate_quant,
    gate_scale,
    up_quant,
    up_scale,
    down_quant,
    down_scale,
):
    depth, side = sizes
    devices = depth * side * 2
    tok_rows, width = tokens.shape
    requests = cache_keys.shape[0]
    me = lax.axis_index("dp")
    z, y, core = me // (2 * side), (me // 2) % side, me % 2

    def place(z, y, core):
        return (z * side + y) * 2 + core

    everyone = [(a, b, c) for a in range(depth) for b in range(side) for c in range(2)]
    next_chip = [(place(a, b, c), place((a + 1) % depth, b, c)) for a, b, c in everyone]
    other_side = [(place(a, b, c), place(a, side - 1 - b, c)) for a, b, c in everyone]
    other_core = [(place(a, b, c), place(a, b, 1 - c)) for a, b, c in everyone]

    def up(value):
        return lax.ppermute(value, "dp", next_chip)

    def across(value):
        return lax.ppermute(value, "dp", other_side)

    routed = expert_ids[:, :, None] == jnp.arange(devices, dtype=jnp.int32)
    weights = jnp.sum(jnp.where(routed, gate_probs[:, :, None], 0.0), 1)
    all_weights = lax.all_gather(weights.T, "dp")

    own = dequant(
        gate_quant[0], gate_scale[0], up_quant[0], up_scale[0], down_quant[0], down_scale[0]
    )
    other = [lax.ppermute(value, "dp", other_core) for value in own]
    columns = jnp.stack([me, place(z, y, 1 - core)])

    def weights_of(back, first, rows):
        from_z = (z - back + depth) % depth
        sides = [y] if side == 1 else [y, 1 - y]
        picked = [
            lax.dynamic_index_in_dim(all_weights, place(from_z, b, core), 0, keepdims=False)
            for b in sides
        ]
        return jnp.concatenate([p[columns, first : first + rows].T for p in picked], 0)

    fixed = (
        prefix_lengths,
        tokens,
        mask_positions[:, None],
        mask_embed[None, :],
        queries,
        new_keys,
        new_values,
        cache_keys,
        cache_values,
        norm_gain[None, :],
    )
    if side == 1:
        resid, normed = attend(0, requests, *fixed)
        (near,) = experts([normed], weights_of(0, 0, tok_rows), own, other)

        def turn(back, carry):
            block, sums = carry
            block = up(block)
            (part,) = experts([block], weights_of(back, 0, tok_rows), own, other)
            return block, add(up(sums), part)

        _, sums = lax.fori_loop(1, depth, turn, (normed, jnp.zeros_like(normed)))
        return (resid + near.astype(F32) + up(sums).astype(F32)).astype(BF16)

    halves = 2
    count = requests // halves
    rows = tok_rows // halves
    resids, columns_of, sides_of = [], [], []
    for half in range(halves):
        resid, normed = attend(half * count, count, *fixed)
        resids.append(resid)
        columns_of.append([normed])
        sides_of.append([across(normed)])
    for back in range(1, depth):
        for half in range(halves):
            block = up(columns_of[half][-1])
            columns_of[half].append(block)
            if half == halves - 1 and back == depth - 1:
                sides_of[half].append(up(sides_of[half][-1]))
            else:
                sides_of[half].append(across(block))
    chain = [None] * halves
    waiting = None
    finals = [None] * halves
    for back in [*range(1, depth), 0]:
        for half in range(halves):
            here, there = experts(
                [columns_of[half][back], sides_of[half][back]],
                weights_of(back, half * rows, rows),
                own,
                other,
            )
            terms = [here]
            if half == halves - 1 and back == 1:
                waiting = there
            else:
                if half == halves - 1 and back == 2:
                    there = add(there, up(waiting))
                terms.append(across(there))
            if back == 0:
                terms = [resids[half], *terms]
            if chain[half] is not None:
                terms.append(up(chain[half]))
            chain[half] = add(*terms)
    return jnp.concatenate(chain, 0)


def solution(mesh):
    in_specs = (
        P(("groups", "dp"), None),
        P(("groups", "dp")),
        P(),
        P(("groups", "dp"), None),
        P(("groups", "dp"), None),
        P(("groups", "dp"), None),
        P(("groups", "dp"), None, None),
        P(("groups", "dp"), None, None),
        P(("groups", "dp")),
        P(("groups", "dp"), None),
        P(("groups", "dp"), None),
        P(),
        P("dp", None, None),
        P("dp", None, None),
        P("dp", None, None),
        P("dp", None, None),
        P("dp", None, None),
        P("dp", None, None),
    )
    out_specs = P(("groups", "dp"), None)
    chips = mesh.shape["dp"] // 2
    sizes = (chips // 2, 2) if chips == 8 else (chips, 1)
    return jax.shard_map(
        functools.partial(shards, sizes),
        mesh=mesh,
        in_specs=in_specs,
        out_specs=out_specs,
        check_vma=False,
    )
```

```python
import functools
import math

import jax
import jax.numpy as jnp
from jax import lax
from jax.experimental import pallas as pl
from jax.experimental.pallas import tpu as pltpu
from jax.sharding import PartitionSpec as P

HD = 128
QB = 128
BF16 = jnp.bfloat16
F32 = jnp.float32
ROUTE = 128
MIB = 1024 * 1024
LIGHT = pl.CostEstimate(flops=1, bytes_accessed=1, transcendentals=0)


def params(mib):
    return pltpu.CompilerParams(vmem_limit_bytes=mib * MIB)


def attend_body(
    first,
    lens_ref,
    tok_ref,
    mask_ref,
    embed_ref,
    query_ref,
    new_key_ref,
    new_value_ref,
    key_ref,
    value_ref,
    gain_ref,
    ids_ref,
    probs_ref,
    resid_ref,
    normed_ref,
):
    block_len, width = tok_ref.shape
    prefix, kv_width = key_ref.shape[1:]
    kv_heads = kv_width // HD
    group = width // HD // kv_heads
    request = first + pl.program_id(0)
    length = lens_ref[request]
    scale = math.log2(math.e) / math.sqrt(HD)
    contract_last = (((1,), (1,)), ((), ()))
    queries = [
        jnp.concatenate(
            [query_ref[:, at * HD : (at + 1) * HD] for at in range(head * group, (head + 1) * group)],
            axis=0,
        )
        for head in range(kv_heads)
    ]

    def over(live):
        position = lax.broadcasted_iota(jnp.int32, (1, live), 1)
        closed = jnp.where(position < length, 0.0, -1e30)
        for head in range(kv_heads):
            lanes = slice(head * HD, (head + 1) * HD)
            query = queries[head]
            far = lax.dot_general(
                query, key_ref[0, :live, lanes], contract_last, preferred_element_type=F32
            )
            near = lax.dot_general(
                query, new_key_ref[:, lanes], contract_last, preferred_element_type=F32
            )
            far = far + closed
            top = jnp.maximum(
                jnp.max(far, axis=1, keepdims=True), jnp.max(near, axis=1, keepdims=True)
            )
            far = jnp.exp2((far - top) * scale)
            near = jnp.exp2((near - top) * scale)
            total = jnp.sum(far, axis=1, keepdims=True) + jnp.sum(near, axis=1, keepdims=True)
            out = jnp.dot(
                far.astype(BF16), value_ref[0, :live, lanes], preferred_element_type=F32
            )
            out = out + jnp.dot(
                near.astype(BF16), new_value_ref[:, lanes], preferred_element_type=F32
            )
            out = (out / total).astype(BF16).astype(F32)
            for g in range(group):
                at = (head * group + g) * HD
                resid_ref[:, at : at + HD] = out[g * block_len : (g + 1) * block_len]

    chunk = min(256, prefix)
    chunks = prefix // chunk
    needed = lax.div(length + (chunk - 1), chunk)
    for number in range(1, chunks + 1):
        low = needed <= number if number == 1 else needed == number

        @pl.when(low)
        def _():
            over(number * chunk)

    tok_rows = mask_ref.shape[0]
    row_at = lax.broadcasted_iota(jnp.int32, (block_len, tok_rows), 0) + request * block_len
    on_row = row_at == lax.broadcasted_iota(jnp.int32, (block_len, tok_rows), 1)
    probs = probs_ref[...]
    high = probs.astype(BF16).astype(F32)
    top_k = ids_ref.shape[0]
    table = jnp.concatenate(
        [
            ids_ref[...].astype(F32),
            high,
            probs - high,
            jnp.broadcast_to(mask_ref[...].reshape(1, tok_rows).astype(F32), (8, tok_rows)),
        ],
        axis=0,
    ).astype(BF16)
    table = lax.dot_general(
        on_row.astype(BF16), table, contract_last, preferred_element_type=F32
    )
    mask = table[:, 3 * top_k : 3 * top_k + 1]
    embed = embed_ref[...].reshape(1, width).astype(F32)
    gain = gain_ref[...].reshape(1, width).astype(F32)
    resid = jnp.where(mask > 0.5, embed, tok_ref[...].astype(F32)) + resid_ref[...]
    mean_square = jnp.mean(resid * resid, axis=1, keepdims=True)
    resid_ref[...] = resid
    normed_ref[:, :width] = (resid * lax.rsqrt(mean_square + 1e-06) * gain).astype(BF16)
    lane = lax.broadcasted_iota(jnp.int32, (block_len, ROUTE), 1)
    lane_id = (lane % (ROUTE // 2)).astype(F32)
    share = jnp.zeros((block_len, ROUTE), F32)
    for k in range(top_k):
        high, low = (table[:, at + k : at + k + 1] for at in (top_k, 2 * top_k))
        share = share + jnp.where(
            lane_id == table[:, k : k + 1], jnp.where(lane < ROUTE // 2, high, low), 0.0
        )
    normed_ref[:, width:] = share.astype(BF16)


def attend(first, count, lens, tokens, mask, embed, queries, new_keys, new_values, keys, values, gain, ids, probs):
    tok_rows, width = tokens.shape
    requests, prefix, kv_width = keys.shape
    block_len = tok_rows // requests

    def rows(cols):
        return pl.BlockSpec((block_len, cols), lambda i, lens: (first + i, 0))

    def cache():
        return pl.BlockSpec((1, prefix, kv_width), lambda i, lens: (first + i, 0, 0))

    def whole(size):
        return pl.BlockSpec((size,), lambda i, lens: (0,))

    def out(cols):
        return pl.BlockSpec((block_len, cols), lambda i, lens: (i, 0))

    scored = count * block_len * width * (prefix + block_len)
    return pl.pallas_call(
        functools.partial(attend_body, first),
        grid_spec=pltpu.PrefetchScalarGridSpec(
            num_scalar_prefetch=1,
            grid=(count,),
            in_specs=[
                rows(width),
                whole(tok_rows),
                whole(width),
                rows(width),
                rows(kv_width),
                rows(kv_width),
                cache(),
                cache(),
                whole(width),
                pl.BlockSpec(ids.shape, lambda i, lens: (0, 0)),
                pl.BlockSpec(ids.shape, lambda i, lens: (0, 0)),
            ],
            out_specs=[out(width), out(width + ROUTE)],
        ),
        out_shape=[
            jax.ShapeDtypeStruct((count * block_len, width), F32),
            jax.ShapeDtypeStruct((count * block_len, width + ROUTE), BF16),
        ],
        compiler_params=params(60 if first == 0 else 24),
        cost_estimate=LIGHT,
        name="attend",
    )(lens, tokens, mask, embed, queries, new_keys, new_values, keys, values, gain, ids, probs)


def scale_blocks(factor_of, quant_ref, out_ref, lead):
    row_count, col_count = quant_ref.shape[1:]
    start = pl.program_id(0) * row_count
    for i in range(row_count // QB):
        rows = pl.ds(pl.multiple_of(start + i * QB, QB), QB)
        for j in range(col_count // QB):
            cols = slice(j * QB, (j + 1) * QB)
            factor = factor_of(pl.program_id(0) * (row_count // QB) + i, j)
            block = quant_ref[0, i * QB : (i + 1) * QB, cols].astype(F32) * factor
            out_ref[(*lead, rows, cols)] = block.astype(BF16)


def dequant_body(gate_s, up_s, down_s, gate_ref, up_ref, down_ref, gate_up_ref, out_down_ref):
    scale_blocks(lambda i, j: gate_s[0, j, i], gate_ref, gate_up_ref, (0,))
    scale_blocks(lambda i, j: up_s[0, j, i], up_ref, gate_up_ref, (1,))
    scale_blocks(lambda i, j: down_s[0, i, j], down_ref, out_down_ref, ())


def dequant(gate, gate_scale, up, up_scale, down, down_scale):
    _, width, hidden = gate.shape
    steps = hidden // QB
    part, down_part = width // steps, hidden // steps
    smem = pl.BlockSpec(memory_space=pltpu.SMEM)
    vmem = pl.BlockSpec(memory_space=pltpu.VMEM)
    tall = pl.BlockSpec((1, part, hidden), lambda i: (0, i, 0))
    return pl.pallas_call(
        dequant_body,
        grid=(steps,),
        in_specs=[
            smem,
            smem,
            smem,
            tall,
            tall,
            pl.BlockSpec((1, down_part, width), lambda i: (0, i, 0)),
        ],
        out_specs=[vmem, vmem],
        out_shape=[
            jax.ShapeDtypeStruct((2, width, hidden), BF16),
            jax.ShapeDtypeStruct((hidden, width), BF16),
        ],
        compiler_params=params(8),
        cost_estimate=LIGHT,
        name="dequant",
    )(gate_scale, up_scale, down_scale, gate, up, down)


def experts_body(blocks, chip_ref, *refs):
    x_refs, refs = refs[:blocks], refs[blocks:]
    weight_refs, refs = refs[:4], refs[4:]
    out_refs, (x_all, total) = refs[:blocks], refs[blocks:]
    rows = x_refs[0].shape[0]
    width = x_all.shape[1]
    lane = lax.broadcasted_iota(jnp.int32, (rows, ROUTE), 1) % (ROUTE // 2)
    for at, ref in enumerate(x_refs):
        x_all[at * rows : (at + 1) * rows] = ref[:, :width]
    for number in range(2):
        gate_up, down = weight_refs[2 * number : 2 * number + 2]
        named = lane == chip_ref[number]
        shares = [jnp.where(named, ref[:, width:].astype(F32), 0.0) for ref in x_refs]
        share = jnp.sum(jnp.concatenate(shares, axis=0), axis=1, keepdims=True)
        hidden_width = down.shape[0]
        tile = min(256, hidden_width)
        for at in range(0, hidden_width, tile):
            cols = slice(at, at + tile)
            x = x_all[...]
            gate = jnp.dot(x, gate_up[0, :, cols], preferred_element_type=F32)
            up = jnp.dot(x, gate_up[1, :, cols], preferred_element_type=F32)
            hidden = (gate * jax.nn.sigmoid(gate) * up * share).astype(BF16)
            part = jnp.dot(hidden, down[cols, :], preferred_element_type=F32)
            if number == 0 and at == 0:
                total[...] = part
            else:
                total[...] += part
    for at, ref in enumerate(out_refs):
        ref[...] = total[at * rows : (at + 1) * rows].astype(BF16)


def experts(xs, chip, own, other):
    rows = xs[0].shape[0]
    width = own[1].shape[1]
    hidden = own[1].shape[0]
    blocks = len(xs)
    all_rows = rows * blocks
    vmem = pl.BlockSpec(memory_space=pltpu.VMEM)
    return pl.pallas_call(
        functools.partial(experts_body, blocks),
        in_specs=[pl.BlockSpec(memory_space=pltpu.SMEM)] + [vmem] * (blocks + 4),
        out_specs=[vmem] * blocks,
        out_shape=[jax.ShapeDtypeStruct((rows, width), BF16)] * blocks,
        scratch_shapes=[pltpu.VMEM((all_rows, width), BF16), pltpu.VMEM((all_rows, width), F32)],
        compiler_params=params(16),
        cost_estimate=LIGHT,
        name="experts",
    )(chip, *xs, *own, *other)


def add(*terms):
    total = terms[0].astype(F32)
    for term in terms[1:]:
        total = total + term.astype(F32)
    return total.astype(BF16)


def shards(
    sizes,
    tokens,
    mask_positions,
    mask_embed,
    queries,
    new_keys,
    new_values,
    cache_keys,
    cache_values,
    prefix_lengths,
    expert_ids,
    gate_probs,
    norm_gain,
    gate_quant,
    gate_scale,
    up_quant,
    up_scale,
    down_quant,
    down_scale,
):
    depth, side = sizes
    devices = depth * side * 2
    tok_rows, width = tokens.shape
    requests = cache_keys.shape[0]
    me = lax.axis_index("dp")

    def place(z, y, core):
        return (z * side + y) * 2 + core

    everyone = [(a, b, c) for a in range(depth) for b in range(side) for c in range(2)]
    next_chip = [(place(a, b, c), place((a + 1) % depth, b, c)) for a, b, c in everyone]
    other_side = [(place(a, b, c), place(a, side - 1 - b, c)) for a, b, c in everyone]
    other_core = [(place(a, b, c), place(a, b, 1 - c)) for a, b, c in everyone]

    def up(value):
        return lax.ppermute(value, "dp", next_chip)

    def across(value):
        return lax.ppermute(value, "dp", other_side)

    gate_scale, up_scale = jnp.swapaxes(gate_scale, 1, 2), jnp.swapaxes(up_scale, 1, 2)
    quantized = (gate_quant, gate_scale, up_quant, up_scale, down_quant, down_scale)
    from_core = [lax.ppermute(value, "dp", other_core) for value in quantized]
    chip = jnp.stack([me, me + 1 - 2 * (me % 2)])

    fixed = (
        prefix_lengths,
        tokens,
        mask_positions,
        mask_embed,
        queries,
        new_keys,
        new_values,
        cache_keys,
        cache_values,
        norm_gain,
        expert_ids.T,
        gate_probs.T,
    )
    if side == 1:
        resid, normed = attend(0, requests, *fixed)
        own, other = dequant(*quantized), dequant(*from_core)
        (near,) = experts([normed], chip, own, other)

        def turn(_, carry):
            block, sums = carry
            block = up(block)
            (part,) = experts([block], chip, own, other)
            return block, add(up(sums), part)

        _, sums = lax.fori_loop(1, depth, turn, (normed, jnp.zeros_like(near)))
        return (resid + near.astype(F32) + up(sums).astype(F32)).astype(BF16)

    halves = 2
    count = requests // halves
    last = halves - 1
    latest = []

    def after(values):
        return lax.optimization_barrier((values, latest[-1]))[0] if latest else values

    def then(function, *values):
        out = function(*after(values))
        latest.append(jax.tree.leaves(out)[0])
        return out

    resids, rows_of, sides_of, parts, sums = {}, {}, {}, {}, {}

    def run_attend(half):
        lens = fixed[0]
        resids[half], normed = then(
            lambda lens: attend(half * count, count, lens, *fixed[1:]), lens
        )
        rows_of[0, half] = normed

    def send(back, half):
        rows = after(rows_of[back, half])
        rows_of[back, half] = rows
        if back < depth - 1:
            rows_of[back + 1, half] = up(rows)
        if (back, half) != (depth - 1, last):
            sides_of[back, half] = across(rows)
        if (back, half) == (depth - 2, last):
            sides_of[back, half] = after(sides_of[back, half])
            sides_of[back + 1, half] = up(sides_of[back, half])

    def run_dequant(values):
        return then(lambda scale: dequant(*values[:5], scale), values[5])

    def run_experts(back, half):
        here, there = then(
            lambda x: experts([x, sides_of[back, half]], chip, own, other), rows_of[back, half]
        )
        if (back, half) == (1, last):
            parts[back, half] = [here]
            sums["held"] = up(there)
        else:
            if (back, half) == (2, last):
                there = then(add, there, sums["held"])
            parts[back, half] = [here, across(there)]

    def run_add(back, half):
        terms = parts[back, half]
        if back != 1:
            terms = terms + [sums[half]]
        if back == 0:
            terms = [resids[half]] + terms
        sums[half] = then(add, *terms)
        if back != 0:
            sums[half] = up(sums[half])

    run_attend(0)
    send(0, 0)
    run_attend(1)
    send(0, 1)
    own = run_dequant(quantized)
    send(1, 0)
    other = run_dequant(from_core)
    send(1, 1)
    send(2, 0)
    run_experts(1, 0)
    send(2, 1)
    run_experts(1, 1)
    send(3, 0)
    run_experts(2, 0)
    run_add(1, 0)
    run_experts(2, 1)
    run_add(1, 1)
    run_experts(3, 0)
    run_add(2, 0)
    run_experts(3, 1)
    run_add(2, 1)
    run_experts(0, 0)
    run_add(3, 0)
    run_experts(0, 1)
    run_add(3, 1)
    run_add(0, 0)
    run_add(0, 1)
    return jnp.concatenate([sums[half] for half in range(halves)], 0)


def solution(mesh):
    in_specs = (
        P(("groups", "dp"), None),
        P(("groups", "dp")),
        P(),
        P(("groups", "dp"), None),
        P(("groups", "dp"), None),
        P(("groups", "dp"), None),
        P(("groups", "dp"), None, None),
        P(("groups", "dp"), None, None),
        P(("groups", "dp")),
        P(("groups", "dp"), None),
        P(("groups", "dp"), None),
        P(),
        P("dp", None, None),
        P("dp", None, None),
        P("dp", None, None),
        P("dp", None, None),
        P("dp", None, None),
        P("dp", None, None),
    )
    out_specs = P(("groups", "dp"), None)
    chips = mesh.shape["dp"] // 2
    sizes = (chips // 2, 2) if chips == 8 else (chips, 1)
    return jax.shard_map(
        functools.partial(shards, sizes),
        mesh=mesh,
        in_specs=in_specs,
        out_specs=out_specs,
        check_vma=False,
    )
```

```python
import functools
import math

import jax
import jax.numpy as jnp
from jax import lax
from jax.experimental import pallas as pl
from jax.experimental.pallas import tpu as pltpu
from jax.sharding import PartitionSpec as P

HD = 128
QB = 128
BF16 = jnp.bfloat16
F32 = jnp.float32
TURN = jax.ShapeDtypeStruct((8, 128), jnp.int32)
ROUTE = 128
MIB = 1024 * 1024
LIGHT = pl.CostEstimate(flops=1, bytes_accessed=1, transcendentals=0)


def params(mib):
    return pltpu.CompilerParams(vmem_limit_bytes=mib * MIB)


def attend_body(
    first,
    count,
    _,
    lens_ref,
    tok_hbm,
    mask_ref,
    embed_ref,
    query_hbm,
    new_key_hbm,
    new_value_hbm,
    key_hbm,
    value_hbm,
    gain_ref,
    ids_ref,
    probs_ref,
    resid_ref,
    normed_ref,
    turn_ref,
    tok_ref,
    query_ref,
    new_key_ref,
    new_value_ref,
    key_ref,
    value_ref,
    sems,
):
    turn_ref[...] = jnp.zeros(TURN.shape, TURN.dtype)
    _, prefix, kv_width = key_ref.shape
    width = tok_ref.shape[1]
    block_len = tok_ref.shape[0] // count
    kv_heads = kv_width // HD
    group = width // HD // kv_heads
    scale = math.log2(math.e) / math.sqrt(HD)
    contract_last = (((1,), (1,)), ((), ()))

    copies = []
    for at in range(count):
        source = pl.ds((first + at) * block_len, block_len)
        rows = pl.ds(at * block_len, block_len)
        pairs = [
            (query_hbm.at[source], query_ref.at[rows]),
            (new_key_hbm.at[source], new_key_ref.at[rows]),
            (key_hbm.at[first + at], key_ref.at[at]),
            (new_value_hbm.at[source], new_value_ref.at[rows]),
            (value_hbm.at[first + at], value_ref.at[at]),
            (tok_hbm.at[source], tok_ref.at[rows]),
        ]
        copies.append(
            [pltpu.make_async_copy(a, b, sems.at[at, n]) for n, (a, b) in enumerate(pairs)]
        )
    for group_of in copies:
        for copy in group_of:
            copy.start()

    tok_rows = mask_ref.shape[0]
    probs = probs_ref[...]
    high_probs = probs.astype(BF16).astype(F32)
    top_k = ids_ref.shape[0]
    table_rows = jnp.concatenate(
        [
            ids_ref[...].astype(F32),
            high_probs,
            probs - high_probs,
            jnp.broadcast_to(mask_ref[...].reshape(1, tok_rows).astype(F32), (8, tok_rows)),
        ],
        axis=0,
    ).astype(BF16)
    all_rows = count * block_len
    row_at = lax.broadcasted_iota(jnp.int32, (all_rows, tok_rows), 0) + first * block_len
    on_row = row_at == lax.broadcasted_iota(jnp.int32, (all_rows, tok_rows), 1)
    table = lax.dot_general(
        on_row.astype(BF16), table_rows, contract_last, preferred_element_type=F32
    )
    lane = lax.broadcasted_iota(jnp.int32, (all_rows, ROUTE), 1)
    lane_id = (lane % (ROUTE // 2)).astype(F32)
    share = jnp.zeros((all_rows, ROUTE), F32)
    for k in range(top_k):
        high, low = (table[:, at + k : at + k + 1] for at in (top_k, 2 * top_k))
        share = share + jnp.where(
            lane_id == table[:, k : k + 1], jnp.where(lane < ROUTE // 2, high, low), 0.0
        )
    normed_ref[:, width:] = share.astype(BF16)
    mask = table[:, 3 * top_k : 3 * top_k + 1]
    embed = embed_ref[...].reshape(1, width).astype(F32)
    gain = gain_ref[...].reshape(1, width).astype(F32)

    for at in range(count):
        rows = slice(at * block_len, (at + 1) * block_len)
        length = lens_ref[first + at]
        for copy in copies[at][:5]:
            copy.wait()
        queries = [
            jnp.concatenate(
                [
                    query_ref[rows, g * HD : (g + 1) * HD]
                    for g in range(head * group, (head + 1) * group)
                ],
                axis=0,
            )
            for head in range(kv_heads)
        ]

        def over(live):
            position = lax.broadcasted_iota(jnp.int32, (1, live), 1)
            closed = jnp.where(position < length, 0.0, -1e30)
            for head in range(kv_heads):
                lanes = slice(head * HD, (head + 1) * HD)
                query = queries[head]
                far = lax.dot_general(
                    query, key_ref[at, :live, lanes], contract_last, preferred_element_type=F32
                )
                near = lax.dot_general(
                    query, new_key_ref[rows, lanes], contract_last, preferred_element_type=F32
                )
                far = far + closed
                top = jnp.maximum(
                    jnp.max(far, axis=1, keepdims=True), jnp.max(near, axis=1, keepdims=True)
                )
                far = jnp.exp2((far - top) * scale)
                near = jnp.exp2((near - top) * scale)
                total = jnp.sum(far, axis=1, keepdims=True) + jnp.sum(near, axis=1, keepdims=True)
                out = jnp.dot(
                    far.astype(BF16), value_ref[at, :live, lanes], preferred_element_type=F32
                )
                out = out + jnp.dot(
                    near.astype(BF16), new_value_ref[rows, lanes], preferred_element_type=F32
                )
                out = (out / total).astype(BF16).astype(F32)
                for g in range(group):
                    start = (head * group + g) * HD
                    resid_ref[rows, start : start + HD] = out[g * block_len : (g + 1) * block_len]

        chunk = min(256, prefix)
        chunks = prefix // chunk
        needed = lax.div(length + (chunk - 1), chunk)
        for number in range(1, chunks + 1):
            fits = needed <= number if number == 1 else needed == number
            pl.when(fits)(functools.partial(over, number * chunk))

        copies[at][5].wait()
        resid = resid_ref[rows] + jnp.where(mask[rows] > 0.5, embed, tok_ref[rows].astype(F32))
        mean_square = jnp.mean(resid * resid, axis=1, keepdims=True)
        resid_ref[rows] = resid
        normed_ref[rows, :width] = (resid * lax.rsqrt(mean_square + 1e-06) * gain).astype(BF16)


def attend(first, count, turn, lens, tokens, mask, embed, queries, new_keys, new_values, keys, values, gain, ids, probs):
    tok_rows, width = tokens.shape
    requests, prefix, kv_width = keys.shape
    rows = tok_rows // requests * count
    smem = pl.BlockSpec(memory_space=pltpu.SMEM)
    vmem = pl.BlockSpec(memory_space=pltpu.VMEM)
    hbm = pl.BlockSpec(memory_space=pltpu.HBM)
    return pl.pallas_call(
        functools.partial(attend_body, first, count),
        in_specs=[hbm, smem, hbm, vmem, vmem, hbm, hbm, hbm, hbm, hbm, vmem, vmem, vmem],
        out_specs=[vmem, vmem, vmem],
        out_shape=[
            jax.ShapeDtypeStruct((rows, width), F32),
            jax.ShapeDtypeStruct((rows, width + ROUTE), BF16),
            TURN,
        ],
        scratch_shapes=[
            pltpu.VMEM((rows, width), BF16),
            pltpu.VMEM((rows, width), BF16),
            pltpu.VMEM((rows, kv_width), BF16),
            pltpu.VMEM((rows, kv_width), BF16),
            pltpu.VMEM((count, prefix, kv_width), BF16),
            pltpu.VMEM((count, prefix, kv_width), BF16),
            pltpu.SemaphoreType.DMA((count, 6)),
        ],
        compiler_params=params(60 if first == 0 else 60),
        cost_estimate=pl.CostEstimate(
            flops=16 * rows * width * prefix,
            bytes_accessed=16 * count * prefix * kv_width + 48 * rows * width,
            transcendentals=rows * width // HD * prefix,
        ),
        name="attend",
    )(turn, lens, tokens, mask, embed, queries, new_keys, new_values, keys, values, gain, ids, probs)


def scale_blocks(factor_of, quant_ref, out_ref):
    row_count, col_count = quant_ref.shape[1:]
    first = pl.program_id(0) * (row_count // QB)
    for i in range(row_count // QB):
        factor = jnp.concatenate(
            [jnp.full((1, QB), factor_of(first + i, j), F32) for j in range(col_count // QB)],
            axis=1,
        )
        rows = pl.ds(pl.multiple_of((first + i) * QB, QB), QB)
        block = quant_ref[0, i * QB : (i + 1) * QB].astype(F32) * factor
        out_ref[rows] = block.astype(BF16)


def dequant_body(_, *refs):
    scales, quants, outs, turn_ref = refs[:2], refs[2:8], refs[8:12], refs[12]
    turn_ref[...] = jnp.zeros(TURN.shape, TURN.dtype)
    for own, scale in enumerate(scales):
        gate, up, down = quants[3 * own : 3 * own + 3]
        gate_up_out, down_out = outs[2 * own : 2 * own + 2]
        tall = scale.shape[1] // 3
        scale_blocks(lambda i, j, ref=scale: ref[0, j, i], gate, gate_up_out.at[0])
        scale_blocks(lambda i, j, ref=scale: ref[0, tall + j, i], up, gate_up_out.at[1])
        scale_blocks(lambda i, j, ref=scale: ref[0, 2 * tall + i, j], down, down_out)


def dequant(turn, own, other):
    _, width, hidden = own[0].shape
    steps = hidden // QB
    smem = pl.BlockSpec(memory_space=pltpu.SMEM)
    vmem = pl.BlockSpec(memory_space=pltpu.VMEM)
    tall = pl.BlockSpec((1, width // steps, hidden), lambda i: (0, i, 0))
    wide = pl.BlockSpec((1, hidden // steps, width), lambda i: (0, i, 0))
    gate_up = jax.ShapeDtypeStruct((2, width, hidden), BF16)
    down = jax.ShapeDtypeStruct((hidden, width), BF16)
    weights = pl.pallas_call(
        dequant_body,
        grid=(steps,),
        in_specs=[pl.BlockSpec(memory_space=pl.ANY)] + [smem] * 2 + [tall, tall, wide] * 2,
        out_specs=[vmem] * 5,
        out_shape=[gate_up, down] * 2 + [TURN],
        compiler_params=params(10),
        cost_estimate=LIGHT,
        name="dequant",
    )(turn, own[3], other[3], *own[:3], *other[:3])
    return weights[:2], weights[2:4], weights[4]


def experts_body(blocks, _, chip_ref, *refs):
    x_refs, refs = refs[:blocks], refs[blocks:]
    weight_refs, refs = refs[:4], refs[4:]
    out_refs, (turn_ref, x_all, total) = refs[:blocks], refs[blocks:]
    turn_ref[...] = jnp.zeros(TURN.shape, TURN.dtype)
    rows = x_refs[0].shape[0]
    width = x_all.shape[1]
    lane = lax.broadcasted_iota(jnp.int32, (rows, ROUTE), 1) % (ROUTE // 2)
    for at, ref in enumerate(x_refs):
        x_all[at * rows : (at + 1) * rows] = ref[:, :width]
    for number in range(2):
        gate_up, down = weight_refs[2 * number : 2 * number + 2]
        named = lane == chip_ref[number]
        shares = [jnp.where(named, ref[:, width:].astype(F32), 0.0) for ref in x_refs]
        share = jnp.sum(jnp.concatenate(shares, axis=0), axis=1, keepdims=True)
        hidden_width = down.shape[0]
        tile = min(256, hidden_width)
        for at in range(0, hidden_width, tile):
            cols = slice(at, at + tile)
            x = x_all[...]
            gate = jnp.dot(x, gate_up[0, :, cols], preferred_element_type=F32)
            up = jnp.dot(x, gate_up[1, :, cols], preferred_element_type=F32)
            hidden = (gate * jax.nn.sigmoid(gate) * up * share).astype(BF16)
            part = jnp.dot(hidden, down[cols, :], preferred_element_type=F32)
            if number == 0 and at == 0:
                total[...] = part
            else:
                total[...] += part
    for at, ref in enumerate(out_refs):
        ref[...] = total[at * rows : (at + 1) * rows].astype(BF16)


def experts(turn, xs, chip, own, other):
    rows = xs[0].shape[0]
    width = own[1].shape[1]
    hidden = own[1].shape[0]
    blocks = len(xs)
    all_rows = rows * blocks
    vmem = pl.BlockSpec(memory_space=pltpu.VMEM)
    return pl.pallas_call(
        functools.partial(experts_body, blocks),
        in_specs=[pl.BlockSpec(memory_space=pl.ANY), pl.BlockSpec(memory_space=pltpu.SMEM)]
        + [vmem] * (blocks + 4),
        out_specs=[vmem] * (blocks + 1),
        out_shape=[jax.ShapeDtypeStruct((rows, width), BF16)] * blocks + [TURN],
        scratch_shapes=[pltpu.VMEM((all_rows, width), BF16), pltpu.VMEM((all_rows, width), F32)],
        compiler_params=params(16),
        cost_estimate=LIGHT,
        name="experts",
    )(turn, chip, *xs, *own, *other)


def add(*terms):
    total = terms[0].astype(F32)
    for term in terms[1:]:
        total = total + term.astype(F32)
    return total.astype(BF16)


def shards(
    sizes,
    tokens,
    mask_positions,
    mask_embed,
    queries,
    new_keys,
    new_values,
    cache_keys,
    cache_values,
    prefix_lengths,
    expert_ids,
    gate_probs,
    norm_gain,
    gate_quant,
    gate_scale,
    up_quant,
    up_scale,
    down_quant,
    down_scale,
):
    depth, side = sizes
    devices = depth * side * 2
    tok_rows, width = tokens.shape
    requests = cache_keys.shape[0]
    me = lax.axis_index("dp")

    def place(z, y, core):
        return (z * side + y) * 2 + core

    everyone = [(a, b, c) for a in range(depth) for b in range(side) for c in range(2)]
    next_chip = [(place(a, b, c), place((a + 1) % depth, b, c)) for a, b, c in everyone]
    other_side = [(place(a, b, c), place(a, side - 1 - b, c)) for a, b, c in everyone]
    other_core = [(place(a, b, c), place(a, b, 1 - c)) for a, b, c in everyone]

    def up(value, name="sums"):
        with jax.named_scope(name + "_along_z"):
            return lax.ppermute(value, "dp", next_chip)

    def across(value, name):
        with jax.named_scope(name + "_along_y"):
            return lax.ppermute(value, "dp", other_side)

    scales = [jnp.swapaxes(gate_scale, 1, 2), jnp.swapaxes(up_scale, 1, 2), down_scale]
    quantized = (gate_quant, up_quant, down_quant, jnp.concatenate(scales, axis=1))
    from_core = [lax.ppermute(value, "dp", other_core) for value in quantized]
    chip = jnp.stack([me, me + 1 - 2 * (me % 2)])

    fixed = (
        prefix_lengths,
        tokens,
        mask_positions,
        mask_embed,
        queries,
        new_keys,
        new_values,
        cache_keys,
        cache_values,
        norm_gain,
        expert_ids.T,
        gate_probs.T,
    )
    turn = jnp.zeros(TURN.shape, TURN.dtype)
    if side == 1:
        resid, normed, turn = attend(0, requests, turn, *fixed)
        own, other, turn = dequant(turn, quantized, from_core)
        near, turn = experts(turn, [normed], chip, own, other)

        def step(_, carry):
            block, sums = carry
            block = up(block)
            part, _ = experts(turn, [block], chip, own, other)
            return block, add(up(sums), part)

        _, sums = lax.fori_loop(1, depth, step, (normed, jnp.zeros_like(near)))
        return (resid + near.astype(F32) + up(sums).astype(F32)).astype(BF16)

    halves = 2
    count = requests // halves
    last = halves - 1
    resids, rows_of, sides_of, parts, sums = {}, {}, {}, {}, {}

    def in_turn(values):
        nonlocal turn
        values, turn = lax.optimization_barrier((values, turn))
        return values

    def landed(*places):
        held = in_turn([where[key] for where, key in places])
        for (where, key), value in zip(places, held):
            where[key] = value

    def landed_part(back, half):
        parts[back, half] = in_turn(parts[back, half])

    def run_attend(half):
        nonlocal turn
        resids[half], rows_of[0, half], turn = attend(half * count, count, turn, *fixed)

    def send_on(back, half):
        rows = rows_of[back, half] = in_turn(rows_of[back, half])
        rows_of[back + 1, half] = up(rows, f"rows_{back + 1}_{half}")

    def send_across(back, half):
        if (back, half) == (depth - 1, last):
            rows = sides_of[back - 1, half] = in_turn(sides_of[back - 1, half])
            sides_of[back, half] = up(rows, f"side_{back}_{half}")
        else:
            rows = rows_of[back, half] = in_turn(rows_of[back, half])
            sides_of[back, half] = across(rows, f"rows_{back}_{half}")

    def run_experts(back, half):
        nonlocal turn
        here, there, turn = experts(
            turn, [rows_of[back, half], sides_of[back, half]], chip, own, other
        )
        parts[back, half] = here, there

    def send_part(back, half):
        here, there = parts[back, half]
        there = in_turn(there)
        if (back, half) == (1, last):
            sums["held"] = up(there, "held")
            parts[back, half] = [here]
        else:
            if (back, half) == (2, last):
                there = add(there, sums["held"])
            parts[back, half] = [here, across(there, f"part_{back}_{half}")]

    def send_sums(back, half):
        terms = list(parts[back, half])
        if back != 1:
            terms.append(sums[half])
        if back == 0:
            terms.append(resids[half])
        sums[half] = add(*in_turn(terms))
        if back != 0:
            sums[half] = up(sums[half], f"sums_{back}_{half}")

    a, b = 0, 1
    run_attend(a)
    send_on(0, a)
    send_across(0, a)
    run_attend(b)
    send_on(0, b)
    send_across(0, b)
    send_on(1, a)
    send_across(1, a)
    landed((sides_of, (0, a)))
    own, other, turn = dequant(turn, quantized, from_core)
    send_on(1, b)
    send_across(1, b)
    send_on(2, a)
    send_across(2, a)
    landed((sides_of, (0, b)))
    run_experts(1, a)
    send_part(1, a)
    send_on(2, b)
    send_across(2, b)
    run_experts(1, b)
    send_part(1, b)
    landed((rows_of, (3, a)))
    send_across(3, a)
    run_experts(2, a)
    send_part(2, a)
    send_sums(1, a)
    landed((rows_of, (3, b)), (sides_of, (2, b)), (sums, "held"))
    send_across(3, b)
    run_experts(2, b)
    send_part(2, b)
    send_sums(1, b)
    run_experts(3, a)
    send_part(3, a)
    landed_part(2, a)
    send_sums(2, a)
    run_experts(3, b)
    send_part(3, b)
    landed_part(2, b)
    send_sums(2, b)
    run_experts(0, a)
    send_part(0, a)
    landed_part(3, a)
    send_sums(3, a)
    run_experts(0, b)
    send_part(0, b)
    send_sums(3, b)
    send_sums(0, a)
    send_sums(0, b)
    return jnp.concatenate([sums[half] for half in range(halves)], 0)


def solution(mesh):
    in_specs = (
        P(("groups", "dp"), None),
        P(("groups", "dp")),
        P(),
        P(("groups", "dp"), None),
        P(("groups", "dp"), None),
        P(("groups", "dp"), None),
        P(("groups", "dp"), None, None),
        P(("groups", "dp"), None, None),
        P(("groups", "dp")),
        P(("groups", "dp"), None),
        P(("groups", "dp"), None),
        P(),
        P("dp", None, None),
        P("dp", None, None),
        P("dp", None, None),
        P("dp", None, None),
        P("dp", None, None),
        P("dp", None, None),
    )
    out_specs = P(("groups", "dp"), None)
    chips = mesh.shape["dp"] // 2
    sizes = (chips // 2, 2) if chips == 8 else (chips, 1)
    return jax.shard_map(
        functools.partial(shards, sizes),
        mesh=mesh,
        in_specs=in_specs,
        out_specs=out_specs,
        check_vma=False,
    )
```

```python
import functools
import math

import jax
import jax.numpy as jnp
from jax import lax
from jax.experimental import pallas as pl
from jax.experimental.pallas import tpu as pltpu
from jax.sharding import PartitionSpec as P

HD = 128
QB = 128
BF16 = jnp.bfloat16
F32 = jnp.float32
TURN = jax.ShapeDtypeStruct((8, 128), jnp.int32)
ROUTE = 128
MIB = 1024 * 1024
LIGHT = pl.CostEstimate(flops=1, bytes_accessed=1, transcendentals=0)


def params(mib):
    return pltpu.CompilerParams(vmem_limit_bytes=mib * MIB)


def attend_body(
    first,
    count,
    _,
    lens_ref,
    tok_hbm,
    mask_ref,
    embed_ref,
    query_hbm,
    new_key_hbm,
    new_value_hbm,
    key_hbm,
    value_hbm,
    gain_ref,
    ids_ref,
    probs_ref,
    resid_ref,
    normed_ref,
    turn_ref,
    tok_ref,
    query_ref,
    new_key_ref,
    new_value_ref,
    key_ref,
    value_ref,
    sems,
):
    turn_ref[...] = jnp.zeros(TURN.shape, TURN.dtype)
    _, prefix, kv_width = key_ref.shape
    width = tok_ref.shape[1]
    block_len = tok_ref.shape[0] // count
    kv_heads = kv_width // HD
    group = width // HD // kv_heads
    scale = math.log2(math.e) / math.sqrt(HD)
    contract_last = (((1,), (1,)), ((), ()))

    copies = []
    for at in range(count):
        source = pl.ds((first + at) * block_len, block_len)
        rows = pl.ds(at * block_len, block_len)
        pairs = [
            (query_hbm.at[source], query_ref.at[rows]),
            (new_key_hbm.at[source], new_key_ref.at[rows]),
            (key_hbm.at[first + at], key_ref.at[at]),
            (new_value_hbm.at[source], new_value_ref.at[rows]),
            (value_hbm.at[first + at], value_ref.at[at]),
            (tok_hbm.at[source], tok_ref.at[rows]),
        ]
        copies.append(
            [pltpu.make_async_copy(a, b, sems.at[at, n]) for n, (a, b) in enumerate(pairs)]
        )
    for group_of in copies:
        for copy in group_of:
            copy.start()

    tok_rows = mask_ref.shape[0]
    probs = probs_ref[...]
    high_probs = probs.astype(BF16).astype(F32)
    top_k = ids_ref.shape[0]
    table_rows = jnp.concatenate(
        [
            ids_ref[...].astype(F32),
            high_probs,
            probs - high_probs,
            jnp.broadcast_to(mask_ref[...].reshape(1, tok_rows).astype(F32), (8, tok_rows)),
        ],
        axis=0,
    ).astype(BF16)
    all_rows = count * block_len
    row_at = lax.broadcasted_iota(jnp.int32, (all_rows, tok_rows), 0) + first * block_len
    on_row = row_at == lax.broadcasted_iota(jnp.int32, (all_rows, tok_rows), 1)
    table = lax.dot_general(
        on_row.astype(BF16), table_rows, contract_last, preferred_element_type=F32
    )
    lane = lax.broadcasted_iota(jnp.int32, (all_rows, ROUTE), 1)
    lane_id = (lane % (ROUTE // 2)).astype(F32)
    share = jnp.zeros((all_rows, ROUTE), F32)
    for k in range(top_k):
        high, low = (table[:, at + k : at + k + 1] for at in (top_k, 2 * top_k))
        share = share + jnp.where(
            lane_id == table[:, k : k + 1], jnp.where(lane < ROUTE // 2, high, low), 0.0
        )
    normed_ref[:, width:] = share.astype(BF16)
    mask = table[:, 3 * top_k : 3 * top_k + 1]
    embed = embed_ref[...].reshape(1, width).astype(F32)
    gain = gain_ref[...].reshape(1, width).astype(F32)

    for at in range(count):
        rows = slice(at * block_len, (at + 1) * block_len)
        length = lens_ref[first + at]
        for copy in copies[at][:5]:
            copy.wait()
        queries = [
            jnp.concatenate(
                [
                    query_ref[rows, g * HD : (g + 1) * HD]
                    for g in range(head * group, (head + 1) * group)
                ],
                axis=0,
            )
            for head in range(kv_heads)
        ]

        def over(live):
            position = lax.broadcasted_iota(jnp.int32, (1, live), 1)
            closed = jnp.where(position < length, 0.0, -1e30)
            for head in range(kv_heads):
                lanes = slice(head * HD, (head + 1) * HD)
                query = queries[head]
                far = lax.dot_general(
                    query, key_ref[at, :live, lanes], contract_last, preferred_element_type=F32
                )
                near = lax.dot_general(
                    query, new_key_ref[rows, lanes], contract_last, preferred_element_type=F32
                )
                far = far + closed
                top = jnp.maximum(
                    jnp.max(far, axis=1, keepdims=True), jnp.max(near, axis=1, keepdims=True)
                )
                far = jnp.exp2((far - top) * scale)
                near = jnp.exp2((near - top) * scale)
                total = jnp.sum(far, axis=1, keepdims=True) + jnp.sum(near, axis=1, keepdims=True)
                out = jnp.dot(
                    far.astype(BF16), value_ref[at, :live, lanes], preferred_element_type=F32
                )
                out = out + jnp.dot(
                    near.astype(BF16), new_value_ref[rows, lanes], preferred_element_type=F32
                )
                out = (out / total).astype(BF16).astype(F32)
                for g in range(group):
                    start = (head * group + g) * HD
                    resid_ref[rows, start : start + HD] = out[g * block_len : (g + 1) * block_len]

        chunk = min(256, prefix)
        chunks = prefix // chunk
        needed = lax.div(length + (chunk - 1), chunk)
        for number in range(1, chunks + 1):
            fits = needed <= number if number == 1 else needed == number
            pl.when(fits)(functools.partial(over, number * chunk))

        copies[at][5].wait()
        resid = resid_ref[rows] + jnp.where(mask[rows] > 0.5, embed, tok_ref[rows].astype(F32))
        mean_square = jnp.mean(resid * resid, axis=1, keepdims=True)
        resid_ref[rows] = resid
        normed_ref[rows, :width] = (resid * lax.rsqrt(mean_square + 1e-06) * gain).astype(BF16)


def attend(first, count, turn, lens, tokens, mask, embed, queries, new_keys, new_values, keys, values, gain, ids, probs):
    tok_rows, width = tokens.shape
    requests, prefix, kv_width = keys.shape
    rows = tok_rows // requests * count
    smem = pl.BlockSpec(memory_space=pltpu.SMEM)
    vmem = pl.BlockSpec(memory_space=pltpu.VMEM)
    hbm = pl.BlockSpec(memory_space=pltpu.HBM)
    return pl.pallas_call(
        functools.partial(attend_body, first, count),
        in_specs=[hbm, smem, hbm, vmem, vmem, hbm, hbm, hbm, hbm, hbm, vmem, vmem, vmem],
        out_specs=[vmem, vmem, vmem],
        out_shape=[
            jax.ShapeDtypeStruct((rows, width), F32),
            jax.ShapeDtypeStruct((rows, width + ROUTE), BF16),
            TURN,
        ],
        scratch_shapes=[
            pltpu.VMEM((rows, width), BF16),
            pltpu.VMEM((rows, width), BF16),
            pltpu.VMEM((rows, kv_width), BF16),
            pltpu.VMEM((rows, kv_width), BF16),
            pltpu.VMEM((count, prefix, kv_width), BF16),
            pltpu.VMEM((count, prefix, kv_width), BF16),
            pltpu.SemaphoreType.DMA((count, 6)),
        ],
        compiler_params=params(60),
        cost_estimate=pl.CostEstimate(
            flops=16 * rows * width * prefix,
            bytes_accessed=16 * count * prefix * kv_width + 48 * rows * width,
            transcendentals=rows * width // HD * prefix,
        ),
        name="attend",
    )(turn, lens, tokens, mask, embed, queries, new_keys, new_values, keys, values, gain, ids, probs)


def scale_blocks(factor_of, quant_ref, out_ref):
    row_count, col_count = quant_ref.shape[1:]
    first = pl.program_id(0) * (row_count // QB)
    for i in range(row_count // QB):
        factor = jnp.concatenate(
            [jnp.full((1, QB), factor_of(first + i, j), F32) for j in range(col_count // QB)],
            axis=1,
        )
        rows = pl.ds(pl.multiple_of((first + i) * QB, QB), QB)
        block = quant_ref[0, i * QB : (i + 1) * QB].astype(F32) * factor
        out_ref[rows] = block.astype(BF16)


def dequant_body(_, *refs):
    scales, quants, outs, turn_ref = refs[:2], refs[2:8], refs[8:12], refs[12]
    turn_ref[...] = jnp.zeros(TURN.shape, TURN.dtype)
    for own, scale in enumerate(scales):
        gate, up, down = quants[3 * own : 3 * own + 3]
        gate_up_out, down_out = outs[2 * own : 2 * own + 2]
        tall = scale.shape[1] // 3
        scale_blocks(lambda i, j, ref=scale: ref[0, j, i], gate, gate_up_out.at[0])
        scale_blocks(lambda i, j, ref=scale: ref[0, tall + j, i], up, gate_up_out.at[1])
        scale_blocks(lambda i, j, ref=scale: ref[0, 2 * tall + i, j], down, down_out)


def dequant(turn, own, other):
    _, width, hidden = own[0].shape
    steps = hidden // QB
    smem = pl.BlockSpec(memory_space=pltpu.SMEM)
    vmem = pl.BlockSpec(memory_space=pltpu.VMEM)
    tall = pl.BlockSpec((1, width // steps, hidden), lambda i: (0, i, 0))
    wide = pl.BlockSpec((1, hidden // steps, width), lambda i: (0, i, 0))
    gate_up = jax.ShapeDtypeStruct((2, width, hidden), BF16)
    down = jax.ShapeDtypeStruct((hidden, width), BF16)
    weights = pl.pallas_call(
        dequant_body,
        grid=(steps,),
        in_specs=[pl.BlockSpec(memory_space=pl.ANY)] + [smem] * 2 + [tall, tall, wide] * 2,
        out_specs=[vmem] * 5,
        out_shape=[gate_up, down] * 2 + [TURN],
        compiler_params=params(10),
        cost_estimate=LIGHT,
        name="dequant",
    )(turn, own[3], other[3], *own[:3], *other[:3])
    return weights[:2], weights[2:4], weights[4]


def experts_body(blocks, _, chip_ref, *refs):
    x_refs, refs = refs[:blocks], refs[blocks:]
    weight_refs, refs = refs[:4], refs[4:]
    out_refs, (turn_ref, x_all, total) = refs[:blocks], refs[blocks:]
    turn_ref[...] = jnp.zeros(TURN.shape, TURN.dtype)
    rows = x_refs[0].shape[0]
    width = x_all.shape[1]
    lane = lax.broadcasted_iota(jnp.int32, (rows, ROUTE), 1) % (ROUTE // 2)
    for at, ref in enumerate(x_refs):
        x_all[at * rows : (at + 1) * rows] = ref[:, :width]
    for number in range(2):
        gate_up, down = weight_refs[2 * number : 2 * number + 2]
        named = lane == chip_ref[number]
        shares = [jnp.where(named, ref[:, width:].astype(F32), 0.0) for ref in x_refs]
        share = jnp.sum(jnp.concatenate(shares, axis=0), axis=1, keepdims=True)
        hidden_width = down.shape[0]
        tile = min(256, hidden_width)
        for at in range(0, hidden_width, tile):
            cols = slice(at, at + tile)
            x = x_all[...]
            gate = jnp.dot(x, gate_up[0, :, cols], preferred_element_type=F32)
            up = jnp.dot(x, gate_up[1, :, cols], preferred_element_type=F32)
            hidden = (gate * jax.nn.sigmoid(gate) * up * share).astype(BF16)
            part = jnp.dot(hidden, down[cols, :], preferred_element_type=F32)
            if number == 0 and at == 0:
                total[...] = part
            else:
                total[...] += part
    for at, ref in enumerate(out_refs):
        ref[...] = total[at * rows : (at + 1) * rows].astype(BF16)


def experts(turn, xs, chip, own, other):
    rows = xs[0].shape[0]
    width = own[1].shape[1]
    hidden = own[1].shape[0]
    blocks = len(xs)
    all_rows = rows * blocks
    vmem = pl.BlockSpec(memory_space=pltpu.VMEM)
    return pl.pallas_call(
        functools.partial(experts_body, blocks),
        in_specs=[pl.BlockSpec(memory_space=pl.ANY), pl.BlockSpec(memory_space=pltpu.SMEM)]
        + [vmem] * (blocks + 4),
        out_specs=[vmem] * (blocks + 1),
        out_shape=[jax.ShapeDtypeStruct((rows, width), BF16)] * blocks + [TURN],
        scratch_shapes=[pltpu.VMEM((all_rows, width), BF16), pltpu.VMEM((all_rows, width), F32)],
        compiler_params=params(16),
        cost_estimate=LIGHT,
        name="experts",
    )(turn, chip, *xs, *own, *other)


def add(*terms):
    total = terms[0].astype(F32)
    for term in terms[1:]:
        total = total + term.astype(F32)
    return total.astype(BF16)


def shards(
    sizes,
    tokens,
    mask_positions,
    mask_embed,
    queries,
    new_keys,
    new_values,
    cache_keys,
    cache_values,
    prefix_lengths,
    expert_ids,
    gate_probs,
    norm_gain,
    gate_quant,
    gate_scale,
    up_quant,
    up_scale,
    down_quant,
    down_scale,
):
    depth, side = sizes
    devices = depth * side * 2
    tok_rows, width = tokens.shape
    requests = cache_keys.shape[0]
    me = lax.axis_index("dp")

    def place(z, y, core):
        return (z * side + y) * 2 + core

    everyone = [(a, b, c) for a in range(depth) for b in range(side) for c in range(2)]
    next_chip = [(place(a, b, c), place((a + 1) % depth, b, c)) for a, b, c in everyone]
    other_side = [(place(a, b, c), place(a, side - 1 - b, c)) for a, b, c in everyone]
    other_core = [(place(a, b, c), place(a, b, 1 - c)) for a, b, c in everyone]

    def up(value, name="sums"):
        with jax.named_scope(name + "_along_z"):
            return lax.ppermute(value, "dp", next_chip)

    def across(value, name):
        with jax.named_scope(name + "_along_y"):
            return lax.ppermute(value, "dp", other_side)

    scales = [jnp.swapaxes(gate_scale, 1, 2), jnp.swapaxes(up_scale, 1, 2), down_scale]
    quantized = (gate_quant, up_quant, down_quant, jnp.concatenate(scales, axis=1))
    chip = jnp.stack([me, me + 1 - 2 * (me % 2)])

    fixed = (
        prefix_lengths,
        tokens,
        mask_positions,
        mask_embed,
        queries,
        new_keys,
        new_values,
        cache_keys,
        cache_values,
        norm_gain,
        expert_ids.T,
        gate_probs.T,
    )
    turn = expert_ids.T
    if side == 1:
        resid, normed, turn = attend(0, requests, turn, *fixed)
        from_core = [lax.ppermute(value, "dp", other_core) for value in quantized]
        own, other, turn = dequant(turn, quantized, from_core)
        near, turn = experts(turn, [normed], chip, own, other)

        def step(_, carry):
            block, sums = carry
            block = up(block)
            part, _ = experts(turn, [block], chip, own, other)
            return block, add(up(sums), part)

        _, sums = lax.fori_loop(1, depth, step, (normed, jnp.zeros_like(near)))
        return (resid + near.astype(F32) + up(sums).astype(F32)).astype(BF16)

    halves = 2
    count = requests // halves
    last = halves - 1
    here, resids, totals = {}, {}, {}

    def in_turn(values):
        nonlocal turn
        values, turn = lax.optimization_barrier((values, turn))
        return values

    from_core = [None] * len(quantized)

    def swap(number):
        from_core[number] = lax.ppermute(in_turn(quantized[number]), "dp", other_core)

    def swapped(number):
        from_core[number] = in_turn(from_core[number])

    def run_attend(half):
        nonlocal turn
        resids[half], here["z", 0, half], turn = attend(half * count, count, turn, *fixed)

    def start(kind, slot, half):
        key = (kind, slot, half)
        route, source = across, key
        if kind == "z":
            route, source = up, ("z", slot - 1, half)
        elif kind == "c":
            route = up
        elif key == ("y", depth - 1, last):
            route, source = up, ("y", slot - 1, half)
        elif kind == "y":
            source = ("z", slot, half)
        elif key == ("r", 1, last):
            route = up
        here[key] = route(in_turn(totals[key] if kind in "rc" else here[source]), f"{kind}{slot}_{half}")

    def land(kind, slot, half):
        key = (kind, slot, half)
        here[key] = in_turn(here[key])

    def run_experts(slot, half):
        nonlocal turn
        mine, totals["r", slot, half], turn = experts(
            turn, [here["z", slot, half], here["y", slot, half]], chip, own, other
        )
        totals["e", slot, half] = mine

    def run_add(slot, half):
        terms = [totals["e", slot, half]]
        if (slot, half) != (1, last):
            terms.append(here["r", slot, half])
        if slot != 1:
            terms.append(here["c", slot - 1 if slot else depth - 1, half])
        if slot == 0:
            terms.append(resids[half])
        totals["c", slot, half] = add(*in_turn(terms))

    def run_held():
        terms = [totals["r", 2, last], here["r", 1, last]]
        totals["r", 2, last] = add(*in_turn(terms))

    a, b = 0, 1
    swap(0)
    swap(1)
    swap(2)
    run_attend(a)
    start("z", 1, a)
    start("y", 0, a)
    swap(3)
    run_attend(b)
    start("z", 1, b)
    swapped(2)
    start("y", 0, b)
    land("z", 1, a)
    swapped(3)
    start("z", 2, a)
    start("y", 1, a)
    land("y", 0, a)
    own, other, turn = dequant(turn, quantized, from_core)
    start("z", 2, b)
    start("y", 1, b)
    land("y", 0, b)
    land("z", 2, a)
    land("y", 1, a)
    start("z", 3, a)
    start("y", 2, a)
    run_experts(1, a)
    start("r", 1, a)
    land("z", 2, b)
    start("z", 3, b)
    start("y", 2, b)
    land("y", 1, b)
    run_experts(1, b)
    start("r", 1, b)
    land("z", 3, a)
    land("y", 2, a)
    start("y", 3, a)
    run_experts(2, a)
    run_add(1, b)
    start("r", 2, a)
    land("r", 1, a)
    run_add(1, a)
    start("c", 1, a)
    land("z", 3, b)
    land("y", 2, b)
    start("y", 3, b)
    run_experts(2, b)
    land("r", 1, b)
    land("y", 3, a)
    run_held()
    land("r", 2, a)
    start("r", 2, b)
    start("c", 1, b)
    run_experts(3, a)
    start("r", 3, a)
    run_add(2, a)
    start("c", 2, a)
    run_experts(3, b)
    start("r", 3, b)
    land("c", 1, b)
    land("r", 2, b)
    run_add(2, b)
    start("c", 2, b)
    run_experts(0, a)
    land("c", 2, a)
    land("r", 3, a)
    run_add(3, a)
    start("c", 3, a)
    run_experts(0, b)
    start("r", 0, b)
    start("r", 0, a)
    land("c", 2, b)
    land("r", 3, b)
    run_add(3, b)
    run_add(0, a)
    land("r", 0, b)
    start("c", 3, b)
    run_add(0, b)
    return jnp.concatenate([totals["c", 0, half] for half in range(halves)], 0)


def solution(mesh):
    in_specs = (
        P(("groups", "dp"), None),
        P(("groups", "dp")),
        P(),
        P(("groups", "dp"), None),
        P(("groups", "dp"), None),
        P(("groups", "dp"), None),
        P(("groups", "dp"), None, None),
        P(("groups", "dp"), None, None),
        P(("groups", "dp")),
        P(("groups", "dp"), None),
        P(("groups", "dp"), None),
        P(),
        P("dp", None, None),
        P("dp", None, None),
        P("dp", None, None),
        P("dp", None, None),
        P("dp", None, None),
        P("dp", None, None),
    )
    out_specs = P(("groups", "dp"), None)
    chips = mesh.shape["dp"] // 2
    sizes = (chips // 2, 2) if chips == 8 else (chips, 1)
    return jax.shard_map(
        functools.partial(shards, sizes),
        mesh=mesh,
        in_specs=in_specs,
        out_specs=out_specs,
        check_vma=False,
    )
```
